32 devices in a mesh: grp: 2 (over x), ad: 16 (over z, y, core).
Axes of the slice: x: 2, y: 2, z: 4, core: 2. Of those that a mesh axis runs over, the one named last changes fastest.
Arguments:
- queries: bfloat16 [1024, 4096], P(('grp', 'ad')), parts along dimension 0, may hold values from -100 to 100
- cached_key_vectors: bfloat16 [1024, 64, 512], P(('grp', 'ad')), parts along dimension 0, may hold values from -4 to 4
- stored_values: bfloat16 [1024, 64, 512], P(('grp', 'ad')), parts along dimension 0, may hold values from -12 to 12
- lengths: int32 [1024], P(('grp', 'ad')), parts along dimension 0, may hold values from 2 to 64, as said below
- request_adapters: int32 [1024], P(('grp', 'ad')), parts along dimension 0, may hold values from 0 to 63, as said below
- output_weight_rows: bfloat16 [4096, 8192], P(None, 'ad'), may hold values from -0.09375 to 0.09375
- adapter_down_maps: bfloat16 [4096, 4096], P(None, 'ad'), may hold values from -0.09375 to 0.09375
- adapter_up_maps: bfloat16 [4096, 8192], P('ad'), may hold values from -0.75 to 0.75
Outputs:
- layer_out: bfloat16 [1024, 8192], P(('grp', 'ad')), parts along dimension 0
The draws below stay inside these ranges and needn't reach their ends.
There are 2 independent parts, one for each index of `grp`. The reference program is written for one: setup_inputs(seed, part) draws one part's arguments, and reference() takes and returns one part's arrays. A program takes and returns all parts, laid end to end along the dimension named above; an argument that names none is the same for every part. Nothing has to cross between parts.
Inputs may be any that keep to these rules, and one draw needn't show every extreme that they name: `lengths`: each device's block of 32 requests holds one of length 64. `request_adapters`: adapter a is held by device a // 4 of ad. Among the 32 requests of one device, each holding device that is named is named by exactly 2 of them; one holding device is named so by every device.
All inputs are finite; a program needn't handle non-finite values.
Results may differ from the reference program's by a relative error of at most 0.014.
Values may be sent and summed in bfloat16 or wider, within the bound.
A program may use at most 128 MiB of HBM per device.

```python
import jax
import jax.numpy as jnp
from jax import lax

MODEL_WIDTH = 8192
LOCAL_HEADS = 32
KV_HEADS = 4
HEAD_SIZE = 128
ADAPTER_RANK = 64
ADP_DEV = 4
CAP = 2
REQ_DEV = 32
CTX = 64
ATTEND_FEATURES = 4096
ADAPTER_TOTAL = 64
REQUESTS = 512


def shared_keys(key):
    key_field = jax.random.normal(key, (REQUESTS, CTX, KV_HEADS * HEAD_SIZE), jnp.float32)
    return jnp.clip(key_field, -4.0, 4.0)


def draw_cached_key_vectors(key, part):
    key_field = shared_keys(key)
    return key_field.astype(jnp.bfloat16)


def draw_queries(key, part):
    key = jax.random.fold_in(key, 5)
    entries = jnp.clip(jax.random.normal(key, (REQUESTS, LOCAL_HEADS * HEAD_SIZE), jnp.float32), -4.0, 4.0)
    return entries.astype(jnp.bfloat16)


def draw_lengths(key, part):
    key = jax.random.fold_in(key, 7)
    blocks = REQUESTS // REQ_DEV
    drawn = jax.random.randint(key, (blocks, REQ_DEV), 2, CTX + 1)
    longest = jax.random.randint(jax.random.fold_in(key, 1), (blocks,), 0, REQ_DEV)
    drawn = jnp.where(jnp.arange(REQ_DEV)[None, :] == longest[:, None], CTX, drawn)
    return drawn.reshape(REQUESTS).astype(jnp.int32)


def draw_request_adapters(key, part):
    key = jax.random.fold_in(key, 9)
    blocks = REQUESTS // REQ_DEV
    custodian_chips = ADAPTER_TOTAL // ADP_DEV
    chosen_count = REQ_DEV // CAP
    demand_ranking_sequence = jax.random.permutation(jax.random.fold_in(key, 1), custodian_chips)
    extra_merit_score = jnp.where(demand_ranking_sequence == 0, 1 << 20, (custodian_chips - demand_ranking_sequence) * 4096 // custodian_chips)
    chance_merit_score = jax.random.randint(jax.random.fold_in(key, 2), (blocks, custodian_chips), 0, 4096)
    keeper_merit_score = (chance_merit_score + extra_merit_score[None, :]) * custodian_chips + jnp.arange(custodian_chips)[None, :]
    unused, picked = lax.top_k(keeper_merit_score, chosen_count)
    owner_rows = jnp.repeat(picked, CAP, axis=1)
    shuffle_score = jax.random.randint(jax.random.fold_in(key, 3), (blocks, REQ_DEV), 0, 1 << 20) * REQ_DEV + jnp.arange(REQ_DEV)[None, :]
    shuffle_order = jnp.argsort(shuffle_score, axis=1)
    owner_rows = jnp.take_along_axis(owner_rows, shuffle_order, axis=1)
    within = jax.random.randint(jax.random.fold_in(key, 4), (blocks, REQ_DEV), 0, ADP_DEV)
    return (owner_rows * ADP_DEV + within).reshape(REQUESTS).astype(jnp.int32)


def block_scale(stream_key, extent, cuts, low, top_value):
    level, own = 1.0, jax.random.fold_in(stream_key, 6)
    for position, blocks in cuts:
        heights = jnp.exp(jax.random.uniform(jax.random.fold_in(own, position), (blocks,), jnp.float32, low / len(cuts), top_value / len(cuts)))
        level = level * jnp.repeat(heights, extent[position] // blocks).reshape([-1 if axis == position else 1 for axis in range(len(extent))])
    return level


def normal_values(stream_key, dims, scale, reach, pieces=(), kind=jnp.bfloat16):
    factor_of = block_scale(stream_key, dims, pieces, -0.22, 0.18) if pieces else 1.0
    entries = jax.random.normal(stream_key, dims, jnp.float32) * scale * factor_of
    return jnp.minimum(jnp.maximum(entries, -reach), reach).astype(kind)


def setup_inputs(seed: int = 0, part: int = 0) -> dict:
    splits = jax.random.split(jax.random.key(seed), 9)
    part_splits = jax.random.split(jax.random.fold_in(splits[8], part), 9)
    queries = draw_queries(jax.random.fold_in(jax.random.fold_in(splits[8], part), 71), part)
    cached_key_vectors = draw_cached_key_vectors(jax.random.fold_in(jax.random.fold_in(splits[8], part), 71), part)
    stored_values = normal_values(part_splits[2], (REQUESTS, CTX, KV_HEADS * HEAD_SIZE), 2.0, 12.0, ((0, 16),))
    lengths = draw_lengths(jax.random.fold_in(jax.random.fold_in(splits[8], part), 71), part)
    request_adapters = draw_request_adapters(jax.random.fold_in(jax.random.fold_in(splits[8], part), 71), part)
    output_weight_rows = normal_values(splits[5], (ATTEND_FEATURES, MODEL_WIDTH), ATTEND_FEATURES ** -0.5, 0.09375, ((1, 16),))
    adapter_down_maps = normal_values(splits[6], (ATTEND_FEATURES, ADAPTER_TOTAL * ADAPTER_RANK), ATTEND_FEATURES ** -0.5, 0.09375, ((1, 16),))
    adapter_up_maps = normal_values(splits[7], (ADAPTER_TOTAL * ADAPTER_RANK, MODEL_WIDTH), ADAPTER_RANK ** -0.5, 0.75, ((0, 16),))
    return dict(queries=queries, cached_key_vectors=cached_key_vectors, stored_values=stored_values, lengths=lengths, request_adapters=request_adapters, output_weight_rows=output_weight_rows, adapter_down_maps=adapter_down_maps, adapter_up_maps=adapter_up_maps)


def attention(queries, cached_key_vectors, stored_values, lengths):
    request_count = queries.shape[0]
    group_size = LOCAL_HEADS // KV_HEADS
    query_heads = queries.reshape(request_count, KV_HEADS, group_size, HEAD_SIZE).astype(jnp.float32)
    key_heads = cached_key_vectors.reshape(request_count, CTX, KV_HEADS, HEAD_SIZE).astype(jnp.float32)
    value_heads = stored_values.reshape(request_count, CTX, KV_HEADS, HEAD_SIZE).astype(jnp.float32)
    scores = jnp.einsum("rkgh,rckh->rkgc", query_heads, key_heads) * (HEAD_SIZE ** -0.5)
    live_mask = (jnp.arange(CTX, dtype=jnp.int32)[None, :] < lengths[:, None])[:, None, None, :]
    scores = jnp.where(live_mask, scores, jnp.float32(-1e30))
    row_max = jnp.max(scores, axis=-1, keepdims=True)
    exp_scores = jnp.where(live_mask, jnp.exp(scores - row_max), jnp.float32(0.0))
    probs = (exp_scores / jnp.sum(exp_scores, axis=-1, keepdims=True)).astype(jnp.bfloat16)
    attended = jnp.einsum("rkgc,rckh->rkgh", probs.astype(jnp.float32), value_heads)
    return attended.reshape(request_count, LOCAL_HEADS * HEAD_SIZE).astype(jnp.bfloat16)


def reference(queries, cached_key_vectors, stored_values, lengths, request_adapters, output_weight_rows, adapter_down_maps, adapter_up_maps):
    attended = attention(queries, cached_key_vectors, stored_values, lengths)
    base_out = jnp.dot(attended, output_weight_rows, preferred_element_type=jnp.float32)
    stacked_down = adapter_down_maps.reshape(LOCAL_HEADS * HEAD_SIZE, ADAPTER_TOTAL, ADAPTER_RANK).transpose(1, 0, 2)
    stacked_up = adapter_up_maps.reshape(ADAPTER_TOTAL, ADAPTER_RANK, MODEL_WIDTH)

    def adapt_block(pair):
        block_rows, block_ids = pair
        reduced_rows = jnp.einsum("ra,rak->rk", block_rows.astype(jnp.float32), stacked_down[block_ids].astype(jnp.float32))
        reduced_rows = reduced_rows.astype(jnp.bfloat16)
        delta_outputs = jnp.einsum("rk,rkd->rd", reduced_rows.astype(jnp.float32), stacked_up[block_ids].astype(jnp.float32))
        return delta_outputs.astype(jnp.bfloat16)

    delta_outputs = lax.map(adapt_block, (attended.reshape(-1, REQ_DEV, LOCAL_HEADS * HEAD_SIZE), request_adapters.reshape(-1, REQ_DEV)))
    delta_outputs = delta_outputs.reshape(REQUESTS, MODEL_WIDTH)
    return (base_out + delta_outputs.astype(jnp.float32)).astype(jnp.bfloat16)
```

```python
import functools

import jax
import jax.numpy as jnp
from jax import lax
from jax.experimental import pallas as pl
from jax.experimental.pallas import tpu as pltpu
from jax.sharding import PartitionSpec as P

LOCAL_HEADS = 32
KV_HEADS = 4
HEAD_SIZE = 128
ADAPTER_RANK = 64
CAP = 2
FOLD = 8
PACK = FOLD * CAP
MESH = pl.DeviceIdType.MESH


def attend(queries, cached_key_vectors, stored_values, lengths):
    request_count, positions, kv_width = cached_key_vectors.shape
    group_size = LOCAL_HEADS // KV_HEADS
    query_heads = queries.reshape(request_count, KV_HEADS, group_size, HEAD_SIZE)
    key_heads = cached_key_vectors.reshape(request_count, positions, KV_HEADS, HEAD_SIZE)
    value_heads = stored_values.reshape(request_count, positions, KV_HEADS, HEAD_SIZE)
    scores = jnp.einsum(
        "rkgh,rckh->rkgc", query_heads, key_heads, preferred_element_type=jnp.float32
    ) * HEAD_SIZE ** (-0.5)
    live_mask = (jnp.arange(positions, dtype=jnp.int32)[None, :] < lengths[:, None])[
        :, None, None, :
    ]
    scores = jnp.where(live_mask, scores, jnp.float32(-1e30))
    row_max = jnp.max(scores, axis=-1, keepdims=True)
    exp_scores = jnp.where(live_mask, jnp.exp(scores - row_max), jnp.float32(0.0))
    probs = (exp_scores / jnp.sum(exp_scores, axis=-1, keepdims=True)).astype(jnp.bfloat16)
    attended = jnp.einsum("rkgc,rckh->rkgh", probs, value_heads, preferred_element_type=jnp.float32)
    return attended.reshape(request_count, LOCAL_HEADS * HEAD_SIZE).astype(jnp.bfloat16)


def iota(shape, axis):
    return lax.broadcasted_iota(jnp.int32, shape, axis)


def project_kernel(
    peers,
    snake,
    ids_row_ref,
    ids_col_ref,
    att_ref,
    w_hbm,
    down_hbm,
    up_hbm,
    out_ref,
    rows,
    w_ref,
    down_ref,
    up_ref,
    codes,
    base_send,
    base_recv,
    delta_send,
    delta_recv,
    load_sem,
    ring_send_sem,
    ring_recv_sem,
    sib_send_sem,
    sib_recv_sem,
    code_send_sem,
    code_recv_sem,
    base_send_sem,
    base_recv_sem,
    delta_send_sem,
    delta_recv_sem,
):
    own_rows, width = att_ref.shape
    half = own_rows // 2
    chips = peers // 2
    hops = chips // 2
    columns = w_ref.shape[1]
    share = down_ref.shape[1] // ADAPTER_RANK
    fold_width = up_ref.shape[1] // FOLD

    loads = [
        pltpu.make_async_copy(src, dst, load_sem.at[i])
        for i, (src, dst) in enumerate(((w_hbm, w_ref), (down_hbm, down_ref), (up_hbm, up_ref)))
    ]
    for load in loads:
        load.start()

    me = lax.axis_index("ad")
    core = lax.rem(me, 2)
    my_chip = me // 2

    def place(chip):
        if not snake:
            return chip
        side = lax.rem(chip, 2)
        return (1 - side) * (chip // 2) + side * (chips - 1 - chip // 2)

    def chip_at(spot):
        spot = lax.rem(spot + 2 * chips, chips)
        if not snake:
            return spot
        side = spot // hops
        return (1 - side) * (2 * spot) + side * (2 * chips - 1 - 2 * spot)

    spot = place(my_chip)
    right = chip_at(spot + 1) * 2 + core
    left = chip_at(spot - 1) * 2 + core
    sibling = my_chip * 2 + 1 - core

    barrier = pltpu.get_barrier_semaphore()

    def greet(step, carry):
        pl.semaphore_signal(
            barrier, inc=1, device_id={"ad": lax.rem(me + step, peers)}, device_id_type=MESH
        )
        return carry

    lax.fori_loop(1, peers, greet, 0)

    ids_row = ids_row_ref[...]
    ids_col = ids_col_ref[...]
    owner_row = ids_row // share
    owner_col = ids_col // share
    same = owner_row == owner_col
    first = iota((own_rows, own_rows), 0)
    second = iota((own_rows, own_rows), 1)
    rank_row = jnp.sum((same & (first < second)).astype(jnp.int32), axis=0, keepdims=True)
    rank_col = jnp.sum((same & (second < first)).astype(jnp.int32), axis=1, keepdims=True)
    slot_col = owner_col * CAP + rank_col
    code_row = (owner_row * CAP + rank_row - owner_row) * share + ids_row
    my_codes = codes.at[pl.ds(pl.multiple_of(me * 8, 8), 8)]
    my_codes[:, :own_rows] = jnp.broadcast_to(code_row, (8, own_rows))
    my_codes[:, own_rows:] = jnp.zeros((8, 128 - own_rows), jnp.int32)
    rows[pl.ds(pl.multiple_of(me * own_rows, own_rows), own_rows), :] = att_ref[...]

    pl.semaphore_wait(barrier, peers - 1)

    def ring_copy(direction, hop, part):
        back = hop - 1
        source = chip_at(spot - back if direction == 0 else spot + back) * 2 + core
        piece = rows.at[pl.ds(pl.multiple_of(source * own_rows + part * half, half), half)]
        index = ((hop - 1) * 2 + direction) * 2 + part
        return pltpu.make_async_remote_copy(
            src_ref=piece,
            dst_ref=piece,
            send_sem=ring_send_sem.at[index],
            recv_sem=ring_recv_sem.at[index],
            device_id={"ad": right if direction == 0 else left},
            device_id_type=MESH,
        )

    def ring_arrival(direction, hop, part):
        source = chip_at(spot - hop if direction == 0 else spot + hop) * 2 + core
        piece = rows.at[pl.ds(pl.multiple_of(source * own_rows + part * half, half), half)]
        index = ((hop - 1) * 2 + direction) * 2 + part
        return pltpu.make_async_remote_copy(
            src_ref=piece,
            dst_ref=piece,
            send_sem=ring_send_sem.at[index],
            recv_sem=ring_recv_sem.at[index],
            device_id={"ad": right if direction == 0 else left},
            device_id_type=MESH,
        )

    def sib_copy(direction, hop, part, their_core):
        source = chip_at(spot - hop if direction == 0 else spot + hop) * 2 + their_core
        piece = rows.at[pl.ds(pl.multiple_of(source * own_rows + part * half, half), half)]
        index = (hop * 2 + direction) * 2 + part
        return pltpu.make_async_remote_copy(
            src_ref=piece,
            dst_ref=piece,
            send_sem=sib_send_sem.at[index],
            recv_sem=sib_recv_sem.at[index],
            device_id={"ad": sibling},
            device_id_type=MESH,
        )

    for part in range(2):
        ring_copy(0, 1, part).start()
        ring_copy(1, 1, part).start()
        sib_copy(0, 0, part, core).start()

    def code_copy(source, target):
        piece = codes.at[pl.ds(pl.multiple_of(source * 8, 8), 8)]
        return pltpu.make_async_remote_copy(
            src_ref=piece,
            dst_ref=piece,
            send_sem=code_send_sem.at[target],
            recv_sem=code_recv_sem.at[source],
            device_id={"ad": target},
            device_id_type=MESH,
        )

    def send_codes(step, carry):
        code_copy(me, lax.rem(me + step, peers)).start()
        return carry

    lax.fori_loop(1, peers, send_codes, 0)

    def base_copy(source, target):
        return pltpu.make_async_remote_copy(
            src_ref=base_send.at[target],
            dst_ref=base_recv.at[source],
            send_sem=base_send_sem.at[target],
            recv_sem=base_recv_sem.at[source],
            device_id={"ad": target},
            device_id_type=MESH,
        )

    def delta_copy(source, target):
        return pltpu.make_async_remote_copy(
            src_ref=delta_send.at[pl.ds(pl.multiple_of(target * PACK, PACK), PACK)],
            dst_ref=delta_recv.at[pl.ds(pl.multiple_of(source * PACK, PACK), PACK)],
            send_sem=delta_send_sem.at[target],
            recv_sem=delta_recv_sem.at[source],
            device_id={"ad": target},
            device_id_type=MESH,
        )

    for load in loads:
        load.wait()

    def each_piece(hop, action):
        for part in range(2):
            for direction in range(2):
                if part == direction:
                    action(direction, part)
                else:
                    pl.when(hop < hops)(functools.partial(action, direction, part))

    def step(hop, carry):
        def arrive(direction, part):
            ring_arrival(direction, hop, part).wait_recv()
            if part == direction:
                pl.when(hop < hops)(lambda: ring_copy(direction, hop + 1, part).start())
            else:
                pl.when(hop < hops - 1)(lambda: ring_copy(direction, hop + 1, part).start())
            sib_copy(direction, hop, part, core).start()

        each_piece(hop, arrive)
        each_piece(hop, lambda d, p: sib_copy(d, hop, p, 1 - core).wait_recv())

        @pl.when(hop == hops)
        def _():
            for part in range(2):
                sib_copy(0, 0, part, 1 - core).wait_recv()

        low = chip_at(spot - lax.rem(hop, hops))
        high = chip_at(spot + hop)
        block = jnp.concatenate(
            [
                rows[pl.ds(pl.multiple_of(chip * 2 * own_rows, 2 * own_rows), 2 * own_rows), :]
                for chip in (low, high)
            ],
            axis=0,
        )
        devices = [low * 2, low * 2 + 1, high * 2, high * 2 + 1]
        shrunk = jnp.dot(block, down_ref[...], preferred_element_type=jnp.float32).astype(
            jnp.bfloat16
        )
        picked = []
        for i, device in enumerate(devices):
            pl.when(device != me)(lambda device=device: code_copy(device, me).wait_recv())
            code = codes[pl.ds(pl.multiple_of(device * 8, 8), 8), :own_rows][:1]
            floor = (me * CAP + lax.rem(iota((PACK, own_rows), 0), CAP)) * share
            pick = (code >= floor) & (code < floor + share)
            local_id = jnp.sum(jnp.where(pick, code - floor, 0), axis=1, keepdims=True)
            chosen = jnp.dot(
                pick.astype(jnp.bfloat16),
                shrunk[i * own_rows : (i + 1) * own_rows],
                preferred_element_type=jnp.float32,
            )
            lane = iota(chosen.shape, 1)
            mine = (lane >= local_id * ADAPTER_RANK) & (lane < (local_id + 1) * ADAPTER_RANK)
            picked.append(jnp.where(mine, chosen, 0.0))
        picked = jnp.concatenate(picked, axis=0)
        fold_of = lax.rem(iota(picked.shape, 0), PACK) // CAP
        total = None
        for fold in range(FOLD):
            term = jnp.dot(
                jnp.where(fold_of == fold, picked, 0.0).astype(jnp.bfloat16),
                up_ref[:, fold * fold_width : (fold + 1) * fold_width],
                preferred_element_type=jnp.float32,
            )
            total = term if total is None else total + term
        total = total.astype(jnp.bfloat16)
        for i, device in enumerate(devices):
            piece = total[i * PACK : (i + 1) * PACK]

            @pl.when(device != me)
            def _():
                delta_send[pl.ds(pl.multiple_of(device * PACK, PACK), PACK), :] = piece
                delta_copy(me, device).start()

            @pl.when(device == me)
            def _():
                delta_recv[pl.ds(pl.multiple_of(device * PACK, PACK), PACK), :] = piece

        base = jnp.dot(block, w_ref[...], preferred_element_type=jnp.float32).astype(jnp.bfloat16)
        for i, device in enumerate(devices):
            piece = base[i * own_rows : (i + 1) * own_rows]

            @pl.when(device != me)
            def _():
                base_send[device] = piece
                base_copy(me, device).start()

            @pl.when(device == me)
            def _():
                base_recv[device] = piece

        return carry

    lax.fori_loop(1, hops + 1, step, 0)

    def collect(offset, carry):
        device = lax.rem(me + offset, peers)
        delta_copy(device, me).wait_recv()
        base_copy(device, me).wait_recv()
        return carry

    lax.fori_loop(1, peers, collect, 0)

    lane = iota((own_rows, peers * PACK), 1)
    lane_slot = (lane // PACK) * CAP + lax.rem(lane, CAP)
    lane_fold = lax.rem(lane, PACK) // CAP
    here = lane_slot == slot_col
    take = jnp.concatenate(
        [(here & (lane_fold == fold)).astype(jnp.bfloat16) for fold in range(FOLD)], axis=0
    )
    deltas = jnp.dot(take, delta_recv[...], preferred_element_type=jnp.float32)
    for device in range(peers):
        fold, start = divmod(device * columns, fold_width)
        out_ref[:, device * columns : (device + 1) * columns] = (
            base_recv[device].astype(jnp.float32)
            + deltas[fold * own_rows : (fold + 1) * own_rows, start : start + columns]
        ).astype(jnp.bfloat16)

    def finish(offset, carry):
        device = lax.rem(me + offset, peers)
        code_copy(me, device).wait_send()
        delta_copy(me, device).wait_send()
        base_copy(me, device).wait_send()
        return carry

    lax.fori_loop(1, peers, finish, 0)

    for part in range(2):
        sib_copy(0, 0, part, core).wait_send()

    def drain(hop, carry):
        def one(direction, part):
            ring_copy(direction, hop, part).wait_send()
            sib_copy(direction, hop, part, core).wait_send()

        each_piece(hop, one)
        return carry

    lax.fori_loop(1, hops + 1, drain, 0)


def project(ids, attended, weights, down, up, snake):
    peers = lax.axis_size("ad")
    own_rows, width = attended.shape
    columns = weights.shape[1]
    hops = peers // 4
    model_width = up.shape[1]
    vmem = pl.BlockSpec(memory_space=pltpu.VMEM)
    hbm = pl.BlockSpec(memory_space=pl.ANY)
    dma = pltpu.SemaphoreType.DMA
    return pl.pallas_call(
        functools.partial(project_kernel, peers, snake),
        out_shape=jax.ShapeDtypeStruct((own_rows, model_width), jnp.bfloat16),
        in_specs=[vmem, vmem, vmem, hbm, hbm, hbm],
        out_specs=vmem,
        scratch_shapes=[
            pltpu.VMEM((peers * own_rows, width), jnp.bfloat16),
            pltpu.VMEM(weights.shape, jnp.bfloat16),
            pltpu.VMEM(down.shape, jnp.bfloat16),
            pltpu.VMEM(up.shape, jnp.bfloat16),
            pltpu.VMEM((peers * 8, 128), jnp.int32),
            pltpu.VMEM((peers, own_rows, columns), jnp.bfloat16),
            pltpu.VMEM((peers, own_rows, columns), jnp.bfloat16),
            pltpu.VMEM((peers * PACK, model_width // FOLD), jnp.bfloat16),
            pltpu.VMEM((peers * PACK, model_width // FOLD), jnp.bfloat16),
            dma((3,)),
            dma((hops * 4,)),
            dma((hops * 4,)),
            dma(((hops + 1) * 4,)),
            dma(((hops + 1) * 4,)),
            dma((peers,)),
            dma((peers,)),
            dma((peers,)),
            dma((peers,)),
            dma((peers,)),
            dma((peers,)),
        ],
        compiler_params=pltpu.CompilerParams(
            collective_id=0, has_side_effects=True, vmem_limit_bytes=56 * 1024 * 1024
        ),
        cost_estimate=pl.CostEstimate(
            flops=2 * peers * own_rows * width * (columns + down.shape[1]),
            bytes_accessed=2 * (weights.size + down.size + up.size),
            transcendentals=0,
        ),
    )(ids.reshape(1, own_rows), ids.reshape(own_rows, 1), attended, weights, down, up)


def local(
    snake,
    queries,
    cached_key_vectors,
    stored_values,
    lengths,
    request_adapters,
    output_weight_rows,
    adapter_down_maps,
    adapter_up_maps,
):
    attended = attend(queries, cached_key_vectors, stored_values, lengths)
    return project(
        request_adapters,
        attended,
        output_weight_rows,
        adapter_down_maps,
        adapter_up_maps,
        snake,
    )


def solution(mesh):
    return jax.shard_map(
        functools.partial(local, mesh.shape["ad"] == 16),
        mesh=mesh,
        in_specs=(
            P(("grp", "ad"), None),
            P(("grp", "ad"), None, None),
            P(("grp", "ad"), None, None),
            P(("grp", "ad")),
            P(("grp", "ad")),
            P(None, "ad"),
            P(None, "ad"),
            P("ad", None),
        ),
        out_specs=P(("grp", "ad"), None),
        check_vma=False,
    )
```

```python
import functools

import jax
import jax.numpy as jnp
from jax import lax
from jax.experimental import pallas as pl
from jax.experimental.pallas import tpu as pltpu
from jax.sharding import PartitionSpec as P

LOCAL_HEADS = 32
KV_HEADS = 4
HEAD_SIZE = 128
ADAPTER_RANK = 64
CAP = 2
FOLD = 8
PACK = FOLD * CAP
MESH = pl.DeviceIdType.MESH


def iota(shape, axis):
    return lax.broadcasted_iota(jnp.int32, shape, axis)


def attend(first, count, lengths_ref, queries_ref, keys, values, heads, out_rows):
    positions, kv_width = keys.shape[1:]
    group_size = LOCAL_HEADS // KV_HEADS
    for head in range(LOCAL_HEADS):
        heads[pl.ds(head, count, stride=LOCAL_HEADS), :] = queries_ref[
            first : first + count, head * HEAD_SIZE : (head + 1) * HEAD_SIZE
        ].astype(jnp.float32)
    batch = 8
    shape = (LOCAL_HEADS, kv_width)
    own_group = iota(shape, 0) // group_size == iota(shape, 1) // HEAD_SIZE

    def some(turn, carry):
        scores, live = [], []
        for i in range(batch):
            place = turn * batch + i
            query = heads[pl.ds(pl.multiple_of(place * LOCAL_HEADS, LOCAL_HEADS), LOCAL_HEADS), :]
            wide = jnp.where(own_group, jnp.concatenate([query] * KV_HEADS, axis=1), 0.0)
            scores.append(
                lax.dot_general(
                    wide.astype(jnp.bfloat16),
                    keys[first + place],
                    (((1,), (1,)), ((), ())),
                    preferred_element_type=jnp.float32,
                )
            )
            live.append(iota((LOCAL_HEADS, positions), 1) < lengths_ref[first + place])
        for i in range(batch):
            place = turn * batch + i
            score = jnp.where(live[i], scores[i] * HEAD_SIZE ** (-0.5), jnp.float32(-1e30))
            row_max = jnp.max(score, axis=-1, keepdims=True)
            weight = jnp.where(live[i], jnp.exp(score - row_max), 0.0)
            probs = (weight / jnp.sum(weight, axis=-1, keepdims=True)).astype(jnp.bfloat16)
            mixed = jnp.dot(probs, values[first + place], preferred_element_type=jnp.float32)
            heads[pl.ds(pl.multiple_of(place * LOCAL_HEADS, LOCAL_HEADS), LOCAL_HEADS), :] = (
                jnp.concatenate(
                    [
                        mixed[
                            g * group_size : (g + 1) * group_size,
                            g * HEAD_SIZE : (g + 1) * HEAD_SIZE,
                        ]
                        for g in range(KV_HEADS)
                    ],
                    axis=0,
                )
            )
        return carry

    lax.fori_loop(0, count // batch, some, 0)
    for head in range(LOCAL_HEADS):
        out_rows[:, head * HEAD_SIZE : (head + 1) * HEAD_SIZE] = heads[
            pl.ds(head, count, stride=LOCAL_HEADS), :
        ].astype(jnp.bfloat16)


def project_kernel(
    peers,
    snake,
    ids_row_ref,
    ids_col_ref,
    lengths_ref,
    queries_ref,
    keys_hbm,
    values_hbm,
    w_hbm,
    down_hbm,
    up_hbm,
    out_ref,
    rows,
    heads,
    keys,
    values,
    w_ref,
    down_ref,
    up_ref,
    codes,
    base_send,
    base_recv,
    delta_send,
    delta_recv,
    load_sem,
    ring_send_sem,
    ring_recv_sem,
    sib_send_sem,
    sib_recv_sem,
    code_send_sem,
    code_recv_sem,
    base_send_sem,
    base_recv_sem,
    delta_send_sem,
    delta_recv_sem,
):
    own_rows, width = queries_ref.shape
    half = own_rows // 2
    chips = peers // 2
    hops = chips // 2
    columns = w_ref.shape[1]
    share = down_ref.shape[1] // ADAPTER_RANK
    fold_width = up_ref.shape[1] // FOLD

    loads = [
        pltpu.make_async_copy(src, dst, load_sem.at[i])
        for i, (src, dst) in enumerate(((w_hbm, w_ref), (down_hbm, down_ref), (up_hbm, up_ref)))
    ]
    cache_loads = [
        pltpu.make_async_copy(
            src.at[pl.ds(part * half, half)],
            dst.at[pl.ds(part * half, half)],
            load_sem.at[3 + part * 2 + i],
        )
        for part in range(2)
        for i, (src, dst) in enumerate(((keys_hbm, keys), (values_hbm, values)))
    ]
    for load in cache_loads + loads:
        load.start()

    me = lax.axis_index("ad")
    core = lax.rem(me, 2)
    my_chip = me // 2

    def place(chip):
        if not snake:
            return chip
        side = lax.rem(chip, 2)
        return (1 - side) * (chip // 2) + side * (chips - 1 - chip // 2)

    def chip_at(spot):
        spot = lax.rem(spot + 2 * chips, chips)
        if not snake:
            return spot
        side = spot // hops
        return (1 - side) * (2 * spot) + side * (2 * chips - 1 - 2 * spot)

    spot = place(my_chip)
    right = chip_at(spot + 1) * 2 + core
    left = chip_at(spot - 1) * 2 + core
    sibling = my_chip * 2 + 1 - core

    barrier = pltpu.get_barrier_semaphore()

    def greet(step, carry):
        pl.semaphore_signal(
            barrier, inc=1, device_id={"ad": lax.rem(me + step, peers)}, device_id_type=MESH
        )
        return carry

    lax.fori_loop(1, peers, greet, 0)

    ids_row = ids_row_ref[...]
    ids_col = ids_col_ref[...]
    owner_row = ids_row // share
    owner_col = ids_col // share
    same = owner_row == owner_col
    first = iota((own_rows, own_rows), 0)
    second = iota((own_rows, own_rows), 1)
    rank_row = jnp.sum((same & (first < second)).astype(jnp.int32), axis=0, keepdims=True)
    rank_col = jnp.sum((same & (second < first)).astype(jnp.int32), axis=1, keepdims=True)
    slot_col = owner_col * CAP + rank_col
    code_row = (owner_row * CAP + rank_row - owner_row) * share + ids_row
    my_codes = codes.at[pl.ds(pl.multiple_of(me * 8, 8), 8)]
    my_codes[:, :own_rows] = jnp.broadcast_to(code_row, (8, own_rows))
    my_codes[:, own_rows:] = jnp.zeros((8, 128 - own_rows), jnp.int32)

    def ring_copy(direction, hop, part):
        back = hop - 1
        source = chip_at(spot - back if direction == 0 else spot + back) * 2 + core
        piece = rows.at[pl.ds(pl.multiple_of(source * own_rows + part * half, half), half)]
        index = ((hop - 1) * 2 + direction) * 2 + part
        return pltpu.make_async_remote_copy(
            src_ref=piece,
            dst_ref=piece,
            send_sem=ring_send_sem.at[index],
            recv_sem=ring_recv_sem.at[index],
            device_id={"ad": right if direction == 0 else left},
            device_id_type=MESH,
        )

    def ring_arrival(direction, hop, part):
        source = chip_at(spot - hop if direction == 0 else spot + hop) * 2 + core
        piece = rows.at[pl.ds(pl.multiple_of(source * own_rows + part * half, half), half)]
        index = ((hop - 1) * 2 + direction) * 2 + part
        return pltpu.make_async_remote_copy(
            src_ref=piece,
            dst_ref=piece,
            send_sem=ring_send_sem.at[index],
            recv_sem=ring_recv_sem.at[index],
            device_id={"ad": right if direction == 0 else left},
            device_id_type=MESH,
        )

    def sib_copy(direction, hop, part, their_core):
        source = chip_at(spot - hop if direction == 0 else spot + hop) * 2 + their_core
        piece = rows.at[pl.ds(pl.multiple_of(source * own_rows + part * half, half), half)]
        index = (hop * 2 + direction) * 2 + part
        return pltpu.make_async_remote_copy(
            src_ref=piece,
            dst_ref=piece,
            send_sem=sib_send_sem.at[index],
            recv_sem=sib_recv_sem.at[index],
            device_id={"ad": sibling},
            device_id_type=MESH,
        )

    for part in range(2):
        for load in cache_loads[part * 2 : part * 2 + 2]:
            load.wait()
        start = pl.multiple_of(me * own_rows + part * half, half)
        attend(
            part * half, half, lengths_ref, queries_ref, keys, values, heads,
            rows.at[pl.ds(start, half)],
        )
        if part == 0:
            pl.semaphore_wait(barrier, peers - 1)
        ring_copy(0, 1, part).start()
        ring_copy(1, 1, part).start()
        sib_copy(0, 0, part, core).start()

    def code_copy(source, target):
        piece = codes.at[pl.ds(pl.multiple_of(source * 8, 8), 8)]
        return pltpu.make_async_remote_copy(
            src_ref=piece,
            dst_ref=piece,
            send_sem=code_send_sem.at[target],
            recv_sem=code_recv_sem.at[source],
            device_id={"ad": target},
            device_id_type=MESH,
        )

    def send_codes(step, carry):
        code_copy(me, lax.rem(me + step, peers)).start()
        return carry

    lax.fori_loop(1, peers, send_codes, 0)

    def base_copy(source, target):
        return pltpu.make_async_remote_copy(
            src_ref=base_send.at[target],
            dst_ref=base_recv.at[source],
            send_sem=base_send_sem.at[target],
            recv_sem=base_recv_sem.at[source],
            device_id={"ad": target},
            device_id_type=MESH,
        )

    def delta_copy(source, target):
        return pltpu.make_async_remote_copy(
            src_ref=delta_send.at[pl.ds(pl.multiple_of(target * PACK, PACK), PACK)],
            dst_ref=delta_recv.at[pl.ds(pl.multiple_of(source * PACK, PACK), PACK)],
            send_sem=delta_send_sem.at[target],
            recv_sem=delta_recv_sem.at[source],
            device_id={"ad": target},
            device_id_type=MESH,
        )

    for load in loads:
        load.wait()

    def each_piece(hop, action):
        for part in range(2):
            for direction in range(2):
                if part == direction:
                    action(direction, part)
                else:
                    pl.when(hop < hops)(functools.partial(action, direction, part))

    def step(hop, carry):
        def arrive(direction, part):
            ring_arrival(direction, hop, part).wait_recv()
            if part == direction:
                pl.when(hop < hops)(lambda: ring_copy(direction, hop + 1, part).start())
            else:
                pl.when(hop < hops - 1)(lambda: ring_copy(direction, hop + 1, part).start())
            sib_copy(direction, hop, part, core).start()

        each_piece(hop, arrive)
        each_piece(hop, lambda d, p: sib_copy(d, hop, p, 1 - core).wait_recv())

        @pl.when(hop == hops)
        def _():
            for part in range(2):
                sib_copy(0, 0, part, 1 - core).wait_recv()

        low = chip_at(spot - lax.rem(hop, hops))
        high = chip_at(spot + hop)
        block = jnp.concatenate(
            [
                rows[pl.ds(pl.multiple_of(chip * 2 * own_rows, 2 * own_rows), 2 * own_rows), :]
                for chip in (low, high)
            ],
            axis=0,
        )
        devices = [low * 2, low * 2 + 1, high * 2, high * 2 + 1]
        shrunk = jnp.dot(block, down_ref[...], preferred_element_type=jnp.float32).astype(
            jnp.bfloat16
        )
        picked = []
        for i, device in enumerate(devices):
            pl.when(device != me)(lambda device=device: code_copy(device, me).wait_recv())
            code = codes[pl.ds(pl.multiple_of(device * 8, 8), 8), :own_rows][:1]
            floor = (me * CAP + lax.rem(iota((PACK, own_rows), 0), CAP)) * share
            pick = (code >= floor) & (code < floor + share)
            local_id = jnp.sum(jnp.where(pick, code - floor, 0), axis=1, keepdims=True)
            chosen = jnp.dot(
                pick.astype(jnp.bfloat16),
                shrunk[i * own_rows : (i + 1) * own_rows],
                preferred_element_type=jnp.float32,
            )
            lane = iota(chosen.shape, 1)
            mine = (lane >= local_id * ADAPTER_RANK) & (lane < (local_id + 1) * ADAPTER_RANK)
            picked.append(jnp.where(mine, chosen, 0.0))
        picked = jnp.concatenate(picked, axis=0)
        fold_of = lax.rem(iota(picked.shape, 0), PACK) // CAP
        total = None
        for fold in range(FOLD):
            term = jnp.dot(
                jnp.where(fold_of == fold, picked, 0.0).astype(jnp.bfloat16),
                up_ref[:, fold * fold_width : (fold + 1) * fold_width],
                preferred_element_type=jnp.float32,
            )
            total = term if total is None else total + term
        total = total.astype(jnp.bfloat16)
        for i, device in enumerate(devices):
            piece = total[i * PACK : (i + 1) * PACK]

            @pl.when(device != me)
            def _():
                delta_send[pl.ds(pl.multiple_of(device * PACK, PACK), PACK), :] = piece
                delta_copy(me, device).start()

            @pl.when(device == me)
            def _():
                delta_recv[pl.ds(pl.multiple_of(device * PACK, PACK), PACK), :] = piece

        base = jnp.dot(block, w_ref[...], preferred_element_type=jnp.float32).astype(jnp.bfloat16)
        for i, device in enumerate(devices):
            piece = base[i * own_rows : (i + 1) * own_rows]

            @pl.when(device != me)
            def _():
                base_send[device] = piece
                base_copy(me, device).start()

            @pl.when(device == me)
            def _():
                base_recv[device] = piece

        return carry

    lax.fori_loop(1, hops + 1, step, 0)

    def collect(offset, carry):
        device = lax.rem(me + offset, peers)
        delta_copy(device, me).wait_recv()
        base_copy(device, me).wait_recv()
        return carry

    lax.fori_loop(1, peers, collect, 0)

    lane = iota((own_rows, peers * PACK), 1)
    lane_slot = (lane // PACK) * CAP + lax.rem(lane, CAP)
    lane_fold = lax.rem(lane, PACK) // CAP
    here = lane_slot == slot_col
    take = jnp.concatenate(
        [(here & (lane_fold == fold)).astype(jnp.bfloat16) for fold in range(FOLD)], axis=0
    )
    deltas = jnp.dot(take, delta_recv[...], preferred_element_type=jnp.float32)
    for device in range(peers):
        fold, start = divmod(device * columns, fold_width)
        out_ref[:, device * columns : (device + 1) * columns] = (
            base_recv[device].astype(jnp.float32)
            + deltas[fold * own_rows : (fold + 1) * own_rows, start : start + columns]
        ).astype(jnp.bfloat16)

    def finish(offset, carry):
        device = lax.rem(me + offset, peers)
        code_copy(me, device).wait_send()
        delta_copy(me, device).wait_send()
        base_copy(me, device).wait_send()
        return carry

    lax.fori_loop(1, peers, finish, 0)

    for part in range(2):
        sib_copy(0, 0, part, core).wait_send()

    def drain(hop, carry):
        def one(direction, part):
            ring_copy(direction, hop, part).wait_send()
            sib_copy(direction, hop, part, core).wait_send()

        each_piece(hop, one)
        return carry

    lax.fori_loop(1, hops + 1, drain, 0)


def project(ids, lengths, queries, keys, values, weights, down, up, snake):
    peers = lax.axis_size("ad")
    own_rows, width = queries.shape
    columns = weights.shape[1]
    hops = peers // 4
    model_width = up.shape[1]
    vmem = pl.BlockSpec(memory_space=pltpu.VMEM)
    smem = pl.BlockSpec(memory_space=pltpu.SMEM)
    hbm = pl.BlockSpec(memory_space=pl.ANY)
    dma = pltpu.SemaphoreType.DMA
    return pl.pallas_call(
        functools.partial(project_kernel, peers, snake),
        out_shape=jax.ShapeDtypeStruct((own_rows, model_width), jnp.bfloat16),
        in_specs=[vmem, vmem, smem, vmem, hbm, hbm, hbm, hbm, hbm],
        out_specs=vmem,
        scratch_shapes=[
            pltpu.VMEM((peers * own_rows, width), jnp.bfloat16),
            pltpu.VMEM((own_rows // 2 * LOCAL_HEADS, HEAD_SIZE), jnp.float32),
            pltpu.VMEM(keys.shape, jnp.bfloat16),
            pltpu.VMEM(values.shape, jnp.bfloat16),
            pltpu.VMEM(weights.shape, jnp.bfloat16),
            pltpu.VMEM(down.shape, jnp.bfloat16),
            pltpu.VMEM(up.shape, jnp.bfloat16),
            pltpu.VMEM((peers * 8, 128), jnp.int32),
            pltpu.VMEM((peers, own_rows, columns), jnp.bfloat16),
            pltpu.VMEM((peers, own_rows, columns), jnp.bfloat16),
            pltpu.VMEM((peers * PACK, model_width // FOLD), jnp.bfloat16),
            pltpu.VMEM((peers * PACK, model_width // FOLD), jnp.bfloat16),
            dma((7,)),
            dma((hops * 4,)),
            dma((hops * 4,)),
            dma(((hops + 1) * 4,)),
            dma(((hops + 1) * 4,)),
            dma((peers,)),
            dma((peers,)),
            dma((peers,)),
            dma((peers,)),
            dma((peers,)),
            dma((peers,)),
        ],
        compiler_params=pltpu.CompilerParams(
            collective_id=0, has_side_effects=True, vmem_limit_bytes=56 * 1024 * 1024
        ),
        cost_estimate=pl.CostEstimate(
            flops=2 * peers * own_rows * width * (columns + down.shape[1]),
            bytes_accessed=2 * (weights.size + down.size + up.size),
            transcendentals=0,
        ),
    )(ids.reshape(1, own_rows), ids.reshape(own_rows, 1), lengths, queries, keys, values, weights, down, up)


def local(
    snake,
    queries,
    cached_key_vectors,
    stored_values,
    lengths,
    request_adapters,
    output_weight_rows,
    adapter_down_maps,
    adapter_up_maps,
):
    return project(
        request_adapters,
        lengths,
        queries,
        cached_key_vectors,
        stored_values,
        output_weight_rows,
        adapter_down_maps,
        adapter_up_maps,
        snake,
    )


def solution(mesh):
    return jax.shard_map(
        functools.partial(local, mesh.shape["ad"] == 16),
        mesh=mesh,
        in_specs=(
            P(("grp", "ad"), None),
            P(("grp", "ad"), None, None),
            P(("grp", "ad"), None, None),
            P(("grp", "ad")),
            P(("grp", "ad")),
            P(None, "ad"),
            P(None, "ad"),
            P("ad", None),
        ),
        out_specs=P(("grp", "ad"), None),
        check_vma=False,
    )
```

```python
import functools

import jax
import jax.numpy as jnp
from jax import lax
from jax.experimental import pallas as pl
from jax.experimental.pallas import tpu as pltpu
from jax.sharding import PartitionSpec as P

LOCAL_HEADS = 32
KV_HEADS = 4
HEAD_SIZE = 128
ADAPTER_RANK = 64
CAP = 2
FOLD = 8
PACK = FOLD * CAP
MESH = pl.DeviceIdType.MESH


def iota(shape, axis):
    return lax.broadcasted_iota(jnp.int32, shape, axis)


def attend(first, count, lengths_ref, queries_ref, keys, values, heads, out_rows):
    positions, kv_width = keys.shape[1:]
    group_size = LOCAL_HEADS // KV_HEADS
    for head in range(LOCAL_HEADS):
        heads[pl.ds(head, count, stride=LOCAL_HEADS), :] = queries_ref[
            first : first + count, head * HEAD_SIZE : (head + 1) * HEAD_SIZE
        ].astype(jnp.float32)
    batch = 8
    shape = (LOCAL_HEADS, kv_width)
    own_group = iota(shape, 0) // group_size == iota(shape, 1) // HEAD_SIZE

    def some(turn, carry):
        scores, live = [], []
        for i in range(batch):
            place = turn * batch + i
            query = heads[pl.ds(pl.multiple_of(place * LOCAL_HEADS, LOCAL_HEADS), LOCAL_HEADS), :]
            wide = jnp.where(own_group, jnp.concatenate([query] * KV_HEADS, axis=1), 0.0)
            scores.append(
                lax.dot_general(
                    wide.astype(jnp.bfloat16),
                    keys[first + place],
                    (((1,), (1,)), ((), ())),
                    preferred_element_type=jnp.float32,
                )
            )
            live.append(iota((LOCAL_HEADS, positions), 1) < lengths_ref[first + place])
        for i in range(batch):
            place = turn * batch + i
            score = jnp.where(live[i], scores[i] * HEAD_SIZE ** (-0.5), jnp.float32(-1e30))
            row_max = jnp.max(score, axis=-1, keepdims=True)
            weight = jnp.where(live[i], jnp.exp(score - row_max), 0.0)
            probs = (weight / jnp.sum(weight, axis=-1, keepdims=True)).astype(jnp.bfloat16)
            mixed = jnp.dot(probs, values[first + place], preferred_element_type=jnp.float32)
            heads[pl.ds(pl.multiple_of(place * LOCAL_HEADS, LOCAL_HEADS), LOCAL_HEADS), :] = (
                jnp.concatenate(
                    [
                        mixed[
                            g * group_size : (g + 1) * group_size,
                            g * HEAD_SIZE : (g + 1) * HEAD_SIZE,
                        ]
                        for g in range(KV_HEADS)
                    ],
                    axis=0,
                )
            )
        return carry

    lax.fori_loop(0, count // batch, some, 0)
    for head in range(LOCAL_HEADS):
        out_rows[:, head * HEAD_SIZE : (head + 1) * HEAD_SIZE] = heads[
            pl.ds(head, count, stride=LOCAL_HEADS), :
        ].astype(jnp.bfloat16)


def project_kernel(
    peers,
    block_2x4,
    ids_row_ref,
    lengths_ref,
    queries_ref,
    keys_hbm,
    values_hbm,
    w_hbm,
    down_hbm,
    up_hbm,
    out_ref,
    rows,
    heads,
    keys,
    values,
    w_ref,
    down_ref,
    up_ref,
    codes,
    base_send,
    base_recv,
    delta_send,
    delta_recv,
    load_sem,
    ring_send_sem,
    ring_recv_sem,
    sib_send_sem,
    sib_recv_sem,
    code_send_sem,
    code_recv_sem,
    base_send_sem,
    base_recv_sem,
    delta_send_sem,
    delta_recv_sem,
):
    own_rows, width = queries_ref.shape
    half = own_rows // 2
    chips = peers // 2
    hops = chips // 2
    columns = w_ref.shape[1]
    share = down_ref.shape[1] // ADAPTER_RANK
    fold_width = up_ref.shape[1] // FOLD

    loads = [
        pltpu.make_async_copy(src, dst, load_sem.at[i])
        for i, (src, dst) in enumerate(((w_hbm, w_ref), (down_hbm, down_ref), (up_hbm, up_ref)))
    ]
    cache_loads = [
        pltpu.make_async_copy(
            src.at[pl.ds(part * half, half)],
            dst.at[pl.ds(part * half, half)],
            load_sem.at[3 + part * 2 + i],
        )
        for part in range(2)
        for i, (src, dst) in enumerate(((keys_hbm, keys), (values_hbm, values)))
    ]
    for load in cache_loads + loads:
        load.start()

    me = lax.axis_index("ad")
    core = lax.rem(me, 2)
    my_chip = me // 2

    def chip_at(spot):
        return lax.rem(spot + 2 * chips, chips)

    spot = my_chip
    right = chip_at(spot + 1) * 2 + core
    left = chip_at(spot - 1) * 2 + core
    sibling = my_chip * 2 + 1 - core

    barrier = pltpu.get_barrier_semaphore()

    def greet(step, carry):
        pl.semaphore_signal(
            barrier, inc=1, device_id={"ad": lax.rem(me + step, peers)}, device_id_type=MESH
        )
        return carry

    lax.fori_loop(1, peers, greet, 0)

    ids_row = ids_row_ref[...]
    owner_row = ids_row // share
    first = iota((own_rows, own_rows), 0)
    second = iota((own_rows, own_rows), 1)
    owner_col = jnp.sum(jnp.where(first == second, owner_row, 0), axis=1, keepdims=True)
    same = owner_row == owner_col
    rank_row = jnp.sum((same & (first < second)).astype(jnp.int32), axis=0, keepdims=True)
    rank_col = jnp.sum((same & (second < first)).astype(jnp.int32), axis=1, keepdims=True)
    slot_col = owner_col * CAP + rank_col
    code_row = (owner_row * CAP + rank_row - owner_row) * share + ids_row
    my_codes = codes.at[pl.ds(pl.multiple_of(me * 8, 8), 8)]
    my_codes[:, :own_rows] = jnp.broadcast_to(code_row, (8, own_rows))
    my_codes[:, own_rows:] = jnp.zeros((8, 128 - own_rows), jnp.int32)

    def ring_copy(direction, hop, part):
        back = hop - 1
        source = chip_at(spot - back if direction == 0 else spot + back) * 2 + core
        piece = rows.at[pl.ds(pl.multiple_of(source * own_rows + part * half, half), half)]
        index = ((hop - 1) * 2 + direction) * 2 + part
        return pltpu.make_async_remote_copy(
            src_ref=piece,
            dst_ref=piece,
            send_sem=ring_send_sem.at[index],
            recv_sem=ring_recv_sem.at[index],
            device_id={"ad": right if direction == 0 else left},
            device_id_type=MESH,
        )

    def ring_arrival(direction, hop, part):
        source = chip_at(spot - hop if direction == 0 else spot + hop) * 2 + core
        piece = rows.at[pl.ds(pl.multiple_of(source * own_rows + part * half, half), half)]
        index = ((hop - 1) * 2 + direction) * 2 + part
        return pltpu.make_async_remote_copy(
            src_ref=piece,
            dst_ref=piece,
            send_sem=ring_send_sem.at[index],
            recv_sem=ring_recv_sem.at[index],
            device_id={"ad": right if direction == 0 else left},
            device_id_type=MESH,
        )

    def sib_copy(direction, hop, part, their_core):
        source = chip_at(spot - hop if direction == 0 else spot + hop) * 2 + their_core
        piece = rows.at[pl.ds(pl.multiple_of(source * own_rows + part * half, half), half)]
        index = (hop * 2 + direction) * 2 + part
        return pltpu.make_async_remote_copy(
            src_ref=piece,
            dst_ref=piece,
            send_sem=sib_send_sem.at[index],
            recv_sem=sib_recv_sem.at[index],
            device_id={"ad": sibling},
            device_id_type=MESH,
        )

    side = lax.rem(my_chip, 2)
    level = my_chip // 2
    last = chips // 2 - 1
    upper = level // 2
    middle = level * (last - level) // 2

    def nearest(turn):
        near = upper * (last - level) + (1 - upper) * level
        near = turn + near * (1 - 2 * turn) * (1 - turn // 2)
        return upper * (last - near) + (1 - upper) * near

    def piece_of(chip, its_core, part):
        start = (chip * 2 + its_core) * own_rows + part * half
        return rows.at[pl.ds(pl.multiple_of(start, half), half)]

    def z_copy(source, up, part):
        piece = piece_of(source * 2 + side, core, part)
        there = lax.rem(level + 1 if up else level + last, last + 1)
        return pltpu.make_async_remote_copy(
            src_ref=piece,
            dst_ref=piece,
            send_sem=ring_send_sem.at[(source + (last + 1 if up else 0)) * 2 + part],
            recv_sem=ring_recv_sem.at[source * 2 + part],
            device_id={"ad": (there * 2 + side) * 2 + core},
            device_id_type=MESH,
        )

    def y_copy(source, its_side, part):
        piece = piece_of(source * 2 + its_side, core, part)
        return pltpu.make_async_remote_copy(
            src_ref=piece,
            dst_ref=piece,
            send_sem=ring_send_sem.at[(source + 2 * (last + 1)) * 2 + part],
            recv_sem=ring_recv_sem.at[(source + last + 1) * 2 + part],
            device_id={"ad": (level * 2 + 1 - side) * 2 + core},
            device_id_type=MESH,
        )

    def twin_copy(chip, part, its_core):
        piece = piece_of(chip, its_core, part)
        return pltpu.make_async_remote_copy(
            src_ref=piece,
            dst_ref=piece,
            send_sem=sib_send_sem.at[chip * 2 + part],
            recv_sem=sib_recv_sem.at[chip * 2 + part],
            device_id={"ad": sibling},
            device_id_type=MESH,
        )

    def z_sends(source, part, action):
        @pl.when((source <= level) & (level < last))
        def _():
            action(z_copy(source, True, part))

        @pl.when((source >= level) & (level > 0))
        def _():
            action(z_copy(source, False, part))

    def pass_on(source, part):
        z_sends(source, part, lambda copy: copy.start())
        y_copy(source, side, part).start()
        twin_copy(source * 2 + side, part, core).start()

    for part in range(2):
        for load in cache_loads[part * 2 : part * 2 + 2]:
            load.wait()
        start = pl.multiple_of(me * own_rows + part * half, half)
        attend(
            part * half, half, lengths_ref, queries_ref, keys, values, heads,
            rows.at[pl.ds(start, half)],
        )
        if part == 0:
            pl.semaphore_wait(barrier, peers - 1)
        if block_2x4:
            pass_on(level, part)
        else:
            ring_copy(0, 1, part).start()
            ring_copy(1, 1, part).start()
            sib_copy(0, 0, part, core).start()

    def code_copy(source, target):
        piece = codes.at[pl.ds(pl.multiple_of(source * 8, 8), 8)]
        return pltpu.make_async_remote_copy(
            src_ref=piece,
            dst_ref=piece,
            send_sem=code_send_sem.at[target],
            recv_sem=code_recv_sem.at[source],
            device_id={"ad": target},
            device_id_type=MESH,
        )

    def send_codes(step, carry):
        code_copy(me, lax.rem(me + step, peers)).start()
        return carry

    lax.fori_loop(1, peers, send_codes, 0)

    def base_copy(source, target):
        return pltpu.make_async_remote_copy(
            src_ref=base_send.at[target],
            dst_ref=base_recv.at[source],
            send_sem=base_send_sem.at[target],
            recv_sem=base_recv_sem.at[source],
            device_id={"ad": target},
            device_id_type=MESH,
        )

    def delta_copy(source, target):
        return pltpu.make_async_remote_copy(
            src_ref=delta_send.at[pl.ds(pl.multiple_of(target * PACK, PACK), PACK)],
            dst_ref=delta_recv.at[pl.ds(pl.multiple_of(source * PACK, PACK), PACK)],
            send_sem=delta_send_sem.at[target],
            recv_sem=delta_recv_sem.at[source],
            device_id={"ad": target},
            device_id_type=MESH,
        )

    for load in loads:
        load.wait()

    def each_piece(hop, action):
        for part in range(2):
            for direction in range(2):
                if part == direction:
                    action(direction, part)
                else:
                    pl.when(hop < hops)(functools.partial(action, direction, part))

    def process(low, high):
        block = jnp.concatenate(
            [
                rows[pl.ds(pl.multiple_of(chip * 2 * own_rows, 2 * own_rows), 2 * own_rows), :]
                for chip in (low, high)
            ],
            axis=0,
        )
        devices = [low * 2, low * 2 + 1, high * 2, high * 2 + 1]
        shrunk = jnp.dot(block, down_ref[...], preferred_element_type=jnp.float32).astype(
            jnp.bfloat16
        )
        picked = []
        for i, device in enumerate(devices):
            pl.when(device != me)(lambda device=device: code_copy(device, me).wait_recv())
            code = codes[pl.ds(pl.multiple_of(device * 8, 8), 8), :own_rows][:1]
            floor = (me * CAP + lax.rem(iota((PACK, own_rows), 0), CAP)) * share
            pick = (code >= floor) & (code < floor + share)
            local_id = jnp.sum(jnp.where(pick, code - floor, 0), axis=1, keepdims=True)
            chosen = jnp.dot(
                pick.astype(jnp.bfloat16),
                shrunk[i * own_rows : (i + 1) * own_rows],
                preferred_element_type=jnp.float32,
            )
            lane = iota(chosen.shape, 1)
            mine = (lane >= local_id * ADAPTER_RANK) & (lane < (local_id + 1) * ADAPTER_RANK)
            picked.append(jnp.where(mine, chosen, 0.0))
        picked = jnp.concatenate(picked, axis=0)
        fold_of = lax.rem(iota(picked.shape, 0), PACK) // CAP
        total = None
        for fold in range(FOLD):
            term = jnp.dot(
                jnp.where(fold_of == fold, picked, 0.0).astype(jnp.bfloat16),
                up_ref[:, fold * fold_width : (fold + 1) * fold_width],
                preferred_element_type=jnp.float32,
            )
            total = term if total is None else total + term
        total = total.astype(jnp.bfloat16)
        for i, device in enumerate(devices):
            piece = total[i * PACK : (i + 1) * PACK]

            @pl.when(device != me)
            def _():
                delta_send[pl.ds(pl.multiple_of(device * PACK, PACK), PACK), :] = piece
                delta_copy(me, device).start()

            @pl.when(device == me)
            def _():
                delta_recv[pl.ds(pl.multiple_of(device * PACK, PACK), PACK), :] = piece

        base = jnp.dot(block, w_ref[...], preferred_element_type=jnp.float32).astype(jnp.bfloat16)
        for i, device in enumerate(devices):
            piece = base[i * own_rows : (i + 1) * own_rows]

            @pl.when(device != me)
            def _():
                base_send[device] = piece
                base_copy(me, device).start()

            @pl.when(device == me)
            def _():
                base_recv[device] = piece

    def step(hop, carry):
        def arrive(direction, part):
            ring_arrival(direction, hop, part).wait_recv()
            if part == direction:
                pl.when(hop < hops)(lambda: ring_copy(direction, hop + 1, part).start())
            else:
                pl.when(hop < hops - 1)(lambda: ring_copy(direction, hop + 1, part).start())
            sib_copy(direction, hop, part, core).start()

        each_piece(hop, arrive)
        each_piece(hop, lambda d, p: sib_copy(d, hop, p, 1 - core).wait_recv())

        @pl.when(hop == hops)
        def _():
            for part in range(2):
                sib_copy(0, 0, part, 1 - core).wait_recv()

        process(chip_at(spot - lax.rem(hop, hops)), chip_at(spot + hop))
        return carry

    def receive(turn):
        source = nearest(turn)
        for part in range(2):
            z_copy(source, True, part).wait_recv()
            pass_on(source, part)

    def line_step(turn, carry):
        ahead = turn + 1 + middle * ((turn + 1) // 2)
        pl.when(ahead <= last)(lambda: receive(ahead))
        pl.when((middle == 1) & (turn == 0))(lambda: receive(2))
        current = nearest(turn)
        for part in range(2):
            y_copy(current, 1 - side, part).wait_recv()
            twin_copy(current * 2 + 1 - side, part, core).start()
        for part in range(2):
            twin_copy(current * 2 + side, part, 1 - core).wait_recv()
            twin_copy(current * 2 + 1 - side, part, 1 - core).wait_recv()
        process(current * 2, current * 2 + 1)
        return carry

    if block_2x4:
        lax.fori_loop(0, last + 1, line_step, 0)
    else:
        lax.fori_loop(1, hops + 1, step, 0)

    def collect(offset, carry):
        device = lax.rem(me + offset, peers)
        delta_copy(device, me).wait_recv()
        base_copy(device, me).wait_recv()
        return carry

    lax.fori_loop(1, peers, collect, 0)

    lane = iota((own_rows, peers * PACK), 1)
    lane_slot = (lane // PACK) * CAP + lax.rem(lane, CAP)
    lane_fold = lax.rem(lane, PACK) // CAP
    here = lane_slot == slot_col
    take = jnp.concatenate(
        [(here & (lane_fold == fold)).astype(jnp.bfloat16) for fold in range(FOLD)], axis=0
    )
    deltas = jnp.dot(take, delta_recv[...], preferred_element_type=jnp.float32)
    for device in range(peers):
        fold, start = divmod(device * columns, fold_width)
        out_ref[:, device * columns : (device + 1) * columns] = (
            base_recv[device].astype(jnp.float32)
            + deltas[fold * own_rows : (fold + 1) * own_rows, start : start + columns]
        ).astype(jnp.bfloat16)

    def finish(offset, carry):
        device = lax.rem(me + offset, peers)
        code_copy(me, device).wait_send()
        delta_copy(me, device).wait_send()
        base_copy(me, device).wait_send()
        return carry

    lax.fori_loop(1, peers, finish, 0)

    def line_drain(source, carry):
        for part in range(2):
            z_sends(source, part, lambda copy: copy.wait_send())
            y_copy(source, side, part).wait_send()
            for its_side in range(2):
                twin_copy(source * 2 + its_side, part, core).wait_send()
        return carry

    if block_2x4:
        lax.fori_loop(0, last + 1, line_drain, 0)
        return

    for part in range(2):
        sib_copy(0, 0, part, core).wait_send()

    def drain(hop, carry):
        def one(direction, part):
            ring_copy(direction, hop, part).wait_send()
            sib_copy(direction, hop, part, core).wait_send()

        each_piece(hop, one)
        return carry

    lax.fori_loop(1, hops + 1, drain, 0)


def project(ids, lengths, queries, keys, values, weights, down, up, block_2x4):
    peers = lax.axis_size("ad")
    own_rows, width = queries.shape
    columns = weights.shape[1]
    hops = peers // 4
    model_width = up.shape[1]
    vmem = pl.BlockSpec(memory_space=pltpu.VMEM)
    smem = pl.BlockSpec(memory_space=pltpu.SMEM)
    hbm = pl.BlockSpec(memory_space=pl.ANY)
    dma = pltpu.SemaphoreType.DMA
    return pl.pallas_call(
        functools.partial(project_kernel, peers, block_2x4),
        out_shape=jax.ShapeDtypeStruct((own_rows, model_width), jnp.bfloat16),
        in_specs=[vmem, smem, vmem, hbm, hbm, hbm, hbm, hbm],
        out_specs=vmem,
        scratch_shapes=[
            pltpu.VMEM((peers * own_rows, width), jnp.bfloat16),
            pltpu.VMEM((own_rows // 2 * LOCAL_HEADS, HEAD_SIZE), jnp.float32),
            pltpu.VMEM(keys.shape, jnp.bfloat16),
            pltpu.VMEM(values.shape, jnp.bfloat16),
            pltpu.VMEM(weights.shape, jnp.bfloat16),
            pltpu.VMEM(down.shape, jnp.bfloat16),
            pltpu.VMEM(up.shape, jnp.bfloat16),
            pltpu.VMEM((peers * 8, 128), jnp.int32),
            pltpu.VMEM((peers, own_rows, columns), jnp.bfloat16),
            pltpu.VMEM((peers, own_rows, columns), jnp.bfloat16),
            pltpu.VMEM((peers * PACK, model_width // FOLD), jnp.bfloat16),
            pltpu.VMEM((peers * PACK, model_width // FOLD), jnp.bfloat16),
            dma((7,)),
            dma((hops * 4 + 8,)),
            dma((hops * 4 + 8,)),
            dma(((hops + 1) * 4,)),
            dma(((hops + 1) * 4,)),
            dma((peers,)),
            dma((peers,)),
            dma((peers,)),
            dma((peers,)),
            dma((peers,)),
            dma((peers,)),
        ],
        compiler_params=pltpu.CompilerParams(
            collective_id=0, has_side_effects=True, vmem_limit_bytes=56 * 1024 * 1024
        ),
        cost_estimate=pl.CostEstimate(
            flops=2 * peers * own_rows * width * (columns + down.shape[1]),
            bytes_accessed=2 * (weights.size + down.size + up.size),
            transcendentals=0,
        ),
    )(ids.reshape(1, own_rows), lengths, queries, keys, values, weights, down, up)


def local(
    block_2x4,
    queries,
    cached_key_vectors,
    stored_values,
    lengths,
    request_adapters,
    output_weight_rows,
    adapter_down_maps,
    adapter_up_maps,
):
    return project(
        request_adapters,
        lengths,
        queries,
        cached_key_vectors,
        stored_values,
        output_weight_rows,
        adapter_down_maps,
        adapter_up_maps,
        block_2x4,
    )


def solution(mesh):
    return jax.shard_map(
        functools.partial(local, mesh.shape["ad"] == 16),
        mesh=mesh,
        in_specs=(
            P(("grp", "ad"), None),
            P(("grp", "ad"), None, None),
            P(("grp", "ad"), None, None),
            P(("grp", "ad")),
            P(("grp", "ad")),
            P(None, "ad"),
            P(None, "ad"),
            P("ad", None),
        ),
        out_specs=P(("grp", "ad"), None),
        check_vma=False,
    )
```

```python
import functools

import jax
import jax.numpy as jnp
from jax import lax
from jax.experimental import pallas as pl
from jax.experimental.pallas import tpu as pltpu
from jax.sharding import PartitionSpec as P

LOCAL_HEADS = 32
KV_HEADS = 4
HEAD_SIZE = 128
ADAPTER_RANK = 64
CAP = 2
FOLD = 8
PACK = FOLD * CAP
MESH = pl.DeviceIdType.MESH


def iota(shape, axis):
    return lax.broadcasted_iota(jnp.int32, shape, axis)


def attend(first, count, lengths_ref, queries_ref, keys, values, heads, out_rows):
    positions, kv_width = keys.shape[1:]
    group_size = LOCAL_HEADS // KV_HEADS
    for head in range(LOCAL_HEADS):
        heads[pl.ds(head, count, stride=LOCAL_HEADS), :] = queries_ref[
            first : first + count, head * HEAD_SIZE : (head + 1) * HEAD_SIZE
        ].astype(jnp.float32)
    batch = 8
    shape = (LOCAL_HEADS, kv_width)
    own_group = iota(shape, 0) // group_size == iota(shape, 1) // HEAD_SIZE

    def some(turn, carry):
        scores, live = [], []
        for i in range(batch):
            place = turn * batch + i
            query = heads[pl.ds(pl.multiple_of(place * LOCAL_HEADS, LOCAL_HEADS), LOCAL_HEADS), :]
            wide = jnp.where(own_group, jnp.concatenate([query] * KV_HEADS, axis=1), 0.0)
            scores.append(
                lax.dot_general(
                    wide.astype(jnp.bfloat16),
                    keys[first + place],
                    (((1,), (1,)), ((), ())),
                    preferred_element_type=jnp.float32,
                )
            )
            live.append(iota((LOCAL_HEADS, positions), 1) < lengths_ref[first + place])
        for i in range(batch):
            place = turn * batch + i
            score = jnp.where(live[i], scores[i] * HEAD_SIZE ** (-0.5), jnp.float32(-1e30))
            row_max = jnp.max(score, axis=-1, keepdims=True)
            weight = jnp.where(live[i], jnp.exp(score - row_max), 0.0)
            probs = (weight / jnp.sum(weight, axis=-1, keepdims=True)).astype(jnp.bfloat16)
            mixed = jnp.dot(probs, values[first + place], preferred_element_type=jnp.float32)
            heads[pl.ds(pl.multiple_of(place * LOCAL_HEADS, LOCAL_HEADS), LOCAL_HEADS), :] = (
                jnp.concatenate(
                    [
                        mixed[
                            g * group_size : (g + 1) * group_size,
                            g * HEAD_SIZE : (g + 1) * HEAD_SIZE,
                        ]
                        for g in range(KV_HEADS)
                    ],
                    axis=0,
                )
            )
        return carry

    lax.fori_loop(0, count // batch, some, 0)
    for head in range(LOCAL_HEADS):
        out_rows[:, head * HEAD_SIZE : (head + 1) * HEAD_SIZE] = heads[
            pl.ds(head, count, stride=LOCAL_HEADS), :
        ].astype(jnp.bfloat16)


def project_kernel(
    peers,
    snake,
    ids_row_ref,
    lengths_ref,
    queries_ref,
    keys_hbm,
    values_hbm,
    w_hbm,
    down_hbm,
    up_hbm,
    out_ref,
    rows,
    heads,
    keys,
    values,
    w_ref,
    down_ref,
    up_ref,
    codes,
    base_send,
    base_recv,
    delta_send,
    delta_recv,
    load_sem,
    ring_send_sem,
    ring_recv_sem,
    sib_send_sem,
    sib_recv_sem,
    code_send_sem,
    code_recv_sem,
    base_send_sem,
    base_recv_sem,
    delta_send_sem,
    delta_recv_sem,
):
    own_rows, width = queries_ref.shape
    half = own_rows // 2
    chips = peers // 2
    hops = chips // 2
    columns = w_ref.shape[1]
    share = down_ref.shape[1] // ADAPTER_RANK
    fold_width = up_ref.shape[1] // FOLD

    loads = [
        pltpu.make_async_copy(src, dst, load_sem.at[i])
        for i, (src, dst) in enumerate(((w_hbm, w_ref), (down_hbm, down_ref), (up_hbm, up_ref)))
    ]
    cache_loads = [
        pltpu.make_async_copy(
            src.at[pl.ds(part * half, half)],
            dst.at[pl.ds(part * half, half)],
            load_sem.at[3 + part * 2 + i],
        )
        for part in range(2)
        for i, (src, dst) in enumerate(((keys_hbm, keys), (values_hbm, values)))
    ]
    for load in cache_loads + loads:
        load.start()

    me = lax.axis_index("ad")
    core = lax.rem(me, 2)
    my_chip = me // 2

    def place(chip):
        if not snake:
            return chip
        side = lax.rem(chip, 2)
        return (1 - side) * (chip // 2) + side * (chips - 1 - chip // 2)

    def chip_at(spot):
        spot = lax.rem(spot + 2 * chips, chips)
        if not snake:
            return spot
        side = spot // hops
        return (1 - side) * (2 * spot) + side * (2 * chips - 1 - 2 * spot)

    spot = place(my_chip)
    right = chip_at(spot + 1) * 2 + core
    left = chip_at(spot - 1) * 2 + core
    sibling = my_chip * 2 + 1 - core

    barrier = pltpu.get_barrier_semaphore()

    def greet(step, carry):
        pl.semaphore_signal(
            barrier, inc=1, device_id={"ad": lax.rem(me + step, peers)}, device_id_type=MESH
        )
        return carry

    lax.fori_loop(1, peers, greet, 0)

    ids_row = ids_row_ref[...]
    owner_row = ids_row // share
    first = iota((own_rows, own_rows), 0)
    second = iota((own_rows, own_rows), 1)
    owner_col = jnp.sum(jnp.where(first == second, owner_row, 0), axis=1, keepdims=True)
    same = owner_row == owner_col
    rank_row = jnp.sum((same & (first < second)).astype(jnp.int32), axis=0, keepdims=True)
    rank_col = jnp.sum((same & (second < first)).astype(jnp.int32), axis=1, keepdims=True)
    slot_col = owner_col * CAP + rank_col
    code_row = (owner_row * CAP + rank_row - owner_row) * share + ids_row
    my_codes = codes.at[pl.ds(pl.multiple_of(me * 8, 8), 8)]
    my_codes[:, :own_rows] = jnp.broadcast_to(code_row, (8, own_rows))
    my_codes[:, own_rows:] = jnp.zeros((8, 128 - own_rows), jnp.int32)

    def ring_copy(direction, hop, part):
        back = hop - 1
        source = chip_at(spot - back if direction == 0 else spot + back) * 2 + core
        piece = rows.at[pl.ds(pl.multiple_of(source * own_rows + part * half, half), half)]
        index = ((hop - 1) * 2 + direction) * 2 + part
        return pltpu.make_async_remote_copy(
            src_ref=piece,
            dst_ref=piece,
            send_sem=ring_send_sem.at[index],
            recv_sem=ring_recv_sem.at[index],
            device_id={"ad": right if direction == 0 else left},
            device_id_type=MESH,
        )

    def ring_arrival(direction, hop, part):
        source = chip_at(spot - hop if direction == 0 else spot + hop) * 2 + core
        piece = rows.at[pl.ds(pl.multiple_of(source * own_rows + part * half, half), half)]
        index = ((hop - 1) * 2 + direction) * 2 + part
        return pltpu.make_async_remote_copy(
            src_ref=piece,
            dst_ref=piece,
            send_sem=ring_send_sem.at[index],
            recv_sem=ring_recv_sem.at[index],
            device_id={"ad": right if direction == 0 else left},
            device_id_type=MESH,
        )

    def sib_copy(direction, hop, part, their_core):
        source = chip_at(spot - hop if direction == 0 else spot + hop) * 2 + their_core
        piece = rows.at[pl.ds(pl.multiple_of(source * own_rows + part * half, half), half)]
        index = (hop * 2 + direction) * 2 + part
        return pltpu.make_async_remote_copy(
            src_ref=piece,
            dst_ref=piece,
            send_sem=sib_send_sem.at[index],
            recv_sem=sib_recv_sem.at[index],
            device_id={"ad": sibling},
            device_id_type=MESH,
        )

    for part in range(2):
        for load in cache_loads[part * 2 : part * 2 + 2]:
            load.wait()
        start = pl.multiple_of(me * own_rows + part * half, half)
        attend(
            part * half, half, lengths_ref, queries_ref, keys, values, heads,
            rows.at[pl.ds(start, half)],
        )
        if part == 0:
            pl.semaphore_wait(barrier, peers - 1)
        ring_copy(0, 1, part).start()
        ring_copy(1, 1, part).start()
        sib_copy(0, 0, part, core).start()

    def code_copy(source, target):
        piece = codes.at[pl.ds(pl.multiple_of(source * 8, 8), 8)]
        return pltpu.make_async_remote_copy(
            src_ref=piece,
            dst_ref=piece,
            send_sem=code_send_sem.at[target],
            recv_sem=code_recv_sem.at[source],
            device_id={"ad": target},
            device_id_type=MESH,
        )

    def send_codes(step, carry):
        code_copy(me, lax.rem(me + step, peers)).start()
        return carry

    lax.fori_loop(1, peers, send_codes, 0)

    def base_copy(source, target):
        return pltpu.make_async_remote_copy(
            src_ref=base_send.at[target],
            dst_ref=base_recv.at[source],
            send_sem=base_send_sem.at[target],
            recv_sem=base_recv_sem.at[source],
            device_id={"ad": target},
            device_id_type=MESH,
        )

    def delta_copy(source, target):
        return pltpu.make_async_remote_copy(
            src_ref=delta_send.at[pl.ds(pl.multiple_of(target * PACK, PACK), PACK)],
            dst_ref=delta_recv.at[pl.ds(pl.multiple_of(source * PACK, PACK), PACK)],
            send_sem=delta_send_sem.at[target],
            recv_sem=delta_recv_sem.at[source],
            device_id={"ad": target},
            device_id_type=MESH,
        )

    for load in loads:
        load.wait()

    def each_piece(hop, action):
        for part in range(2):
            for direction in range(2):
                if part == direction:
                    action(direction, part)
                else:
                    pl.when(hop < hops)(functools.partial(action, direction, part))

    def step(hop, carry):
        def arrive(direction, part):
            ring_arrival(direction, hop, part).wait_recv()
            if part == direction:
                pl.when(hop < hops)(lambda: ring_copy(direction, hop + 1, part).start())
            else:
                pl.when(hop < hops - 1)(lambda: ring_copy(direction, hop + 1, part).start())
            sib_copy(direction, hop, part, core).start()

        each_piece(hop, arrive)
        each_piece(hop, lambda d, p: sib_copy(d, hop, p, 1 - core).wait_recv())

        @pl.when(hop == hops)
        def _():
            for part in range(2):
                sib_copy(0, 0, part, 1 - core).wait_recv()

        low = chip_at(spot - lax.rem(hop, hops))
        high = chip_at(spot + hop)
        block = jnp.concatenate(
            [
                rows[pl.ds(pl.multiple_of(chip * 2 * own_rows, 2 * own_rows), 2 * own_rows), :]
                for chip in (low, high)
            ],
            axis=0,
        )
        devices = [low * 2, low * 2 + 1, high * 2, high * 2 + 1]
        shrunk = jnp.dot(block, down_ref[...], preferred_element_type=jnp.float32).astype(
            jnp.bfloat16
        )
        picked = []
        for i, device in enumerate(devices):
            pl.when(device != me)(lambda device=device: code_copy(device, me).wait_recv())
            code = codes[pl.ds(pl.multiple_of(device * 8, 8), 8), :own_rows][:1]
            floor = (me * CAP + lax.rem(iota((PACK, own_rows), 0), CAP)) * share
            pick = (code >= floor) & (code < floor + share)
            local_id = jnp.sum(jnp.where(pick, code - floor, 0), axis=1, keepdims=True)
            chosen = jnp.dot(
                pick.astype(jnp.bfloat16),
                shrunk[i * own_rows : (i + 1) * own_rows],
                preferred_element_type=jnp.float32,
            )
            lane = iota(chosen.shape, 1)
            mine = (lane >= local_id * ADAPTER_RANK) & (lane < (local_id + 1) * ADAPTER_RANK)
            picked.append(jnp.where(mine, chosen, 0.0))
        picked = jnp.concatenate(picked, axis=0)
        fold_of = lax.rem(iota(picked.shape, 0), PACK) // CAP
        total = None
        for fold in range(FOLD):
            term = jnp.dot(
                jnp.where(fold_of == fold, picked, 0.0).astype(jnp.bfloat16),
                up_ref[:, fold * fold_width : (fold + 1) * fold_width],
                preferred_element_type=jnp.float32,
            )
            total = term if total is None else total + term
        total = total.astype(jnp.bfloat16)
        for i, device in enumerate(devices):
            piece = total[i * PACK : (i + 1) * PACK]

            @pl.when(device != me)
            def _():
                delta_send[pl.ds(pl.multiple_of(device * PACK, PACK), PACK), :] = piece
                delta_copy(me, device).start()

            @pl.when(device == me)
            def _():
                delta_recv[pl.ds(pl.multiple_of(device * PACK, PACK), PACK), :] = piece

        base = jnp.dot(block, w_ref[...], preferred_element_type=jnp.float32).astype(jnp.bfloat16)
        for i, device in enumerate(devices):
            piece = base[i * own_rows : (i + 1) * own_rows]

            @pl.when(device != me)
            def _():
                base_send[device] = piece
                base_copy(me, device).start()

            @pl.when(device == me)
            def _():
                base_recv[device] = piece

        return carry

    lax.fori_loop(1, hops + 1, step, 0)

    def collect(offset, carry):
        device = lax.rem(me + offset, peers)
        delta_copy(device, me).wait_recv()
        base_copy(device, me).wait_recv()
        return carry

    lax.fori_loop(1, peers, collect, 0)

    lane = iota((own_rows, peers * PACK), 1)
    lane_slot = (lane // PACK) * CAP + lax.rem(lane, CAP)
    lane_fold = lax.rem(lane, PACK) // CAP
    here = lane_slot == slot_col
    take = jnp.concatenate(
        [(here & (lane_fold == fold)).astype(jnp.bfloat16) for fold in range(FOLD)], axis=0
    )
    deltas = jnp.dot(take, delta_recv[...], preferred_element_type=jnp.float32)
    for device in range(peers):
        fold, start = divmod(device * columns, fold_width)
        out_ref[:, device * columns : (device + 1) * columns] = (
            base_recv[device].astype(jnp.float32)
            + deltas[fold * own_rows : (fold + 1) * own_rows, start : start + columns]
        ).astype(jnp.bfloat16)

    def finish(offset, carry):
        device = lax.rem(me + offset, peers)
        code_copy(me, device).wait_send()
        delta_copy(me, device).wait_send()
        base_copy(me, device).wait_send()
        return carry

    lax.fori_loop(1, peers, finish, 0)

    for part in range(2):
        sib_copy(0, 0, part, core).wait_send()

    def drain(hop, carry):
        def one(direction, part):
            ring_copy(direction, hop, part).wait_send()
            sib_copy(direction, hop, part, core).wait_send()

        each_piece(hop, one)
        return carry

    lax.fori_loop(1, hops + 1, drain, 0)


def project(ids, lengths, queries, keys, values, weights, down, up, snake):
    peers = lax.axis_size("ad")
    own_rows, width = queries.shape
    columns = weights.shape[1]
    hops = peers // 4
    model_width = up.shape[1]
    vmem = pl.BlockSpec(memory_space=pltpu.VMEM)
    smem = pl.BlockSpec(memory_space=pltpu.SMEM)
    hbm = pl.BlockSpec(memory_space=pl.ANY)
    dma = pltpu.SemaphoreType.DMA
    return pl.pallas_call(
        functools.partial(project_kernel, peers, snake),
        out_shape=jax.ShapeDtypeStruct((own_rows, model_width), jnp.bfloat16),
        in_specs=[vmem, smem, vmem, hbm, hbm, hbm, hbm, hbm],
        out_specs=vmem,
        scratch_shapes=[
            pltpu.VMEM((peers * own_rows, width), jnp.bfloat16),
            pltpu.VMEM((own_rows // 2 * LOCAL_HEADS, HEAD_SIZE), jnp.float32),
            pltpu.VMEM(keys.shape, jnp.bfloat16),
            pltpu.VMEM(values.shape, jnp.bfloat16),
            pltpu.VMEM(weights.shape, jnp.bfloat16),
            pltpu.VMEM(down.shape, jnp.bfloat16),
            pltpu.VMEM(up.shape, jnp.bfloat16),
            pltpu.VMEM((peers * 8, 128), jnp.int32),
            pltpu.VMEM((peers, own_rows, columns), jnp.bfloat16),
            pltpu.VMEM((peers, own_rows, columns), jnp.bfloat16),
            pltpu.VMEM((peers * PACK, model_width // FOLD), jnp.bfloat16),
            pltpu.VMEM((peers * PACK, model_width // FOLD), jnp.bfloat16),
            dma((7,)),
            dma((hops * 4,)),
            dma((hops * 4,)),
            dma(((hops + 1) * 4,)),
            dma(((hops + 1) * 4,)),
            dma((peers,)),
            dma((peers,)),
            dma((peers,)),
            dma((peers,)),
            dma((peers,)),
            dma((peers,)),
        ],
        compiler_params=pltpu.CompilerParams(
            collective_id=0, has_side_effects=True, vmem_limit_bytes=56 * 1024 * 1024
        ),
        cost_estimate=pl.CostEstimate(
            flops=2 * peers * own_rows * width * (columns + down.shape[1]),
            bytes_accessed=2 * (weights.size + down.size + up.size),
            transcendentals=0,
        ),
    )(ids.reshape(1, own_rows), lengths, queries, keys, values, weights, down, up)


def local(
    snake,
    queries,
    cached_key_vectors,
    stored_values,
    lengths,
    request_adapters,
    output_weight_rows,
    adapter_down_maps,
    adapter_up_maps,
):
    return project(
        request_adapters,
        lengths,
        queries,
        cached_key_vectors,
        stored_values,
        output_weight_rows,
        adapter_down_maps,
        adapter_up_maps,
        snake,
    )


def solution(mesh):
    return jax.shard_map(
        functools.partial(local, mesh.shape["ad"] == 16),
        mesh=mesh,
        in_specs=(
            P(("grp", "ad"), None),
            P(("grp", "ad"), None, None),
            P(("grp", "ad"), None, None),
            P(("grp", "ad")),
            P(("grp", "ad")),
            P(None, "ad"),
            P(None, "ad"),
            P("ad", None),
        ),
        out_specs=P(("grp", "ad"), None),
        check_vma=False,
    )
```
